128 devices in a mesh: seq: 32 (over x, y, core), head: 4 (over z).
Axes of the slice: x: 4, y: 4, z: 4, core: 2. Of those that a mesh axis runs over, the one named last changes fastest.
Arguments:
- byte_ids: int32 [32768], P('seq'), may hold values from 0 to 255
- prefix_len: int32 [512], replicated, may hold values from 1 to 32768, as said below
- embed_table: bfloat16 [256, 2048], replicated, may hold values from -6 to 6
- latents: bfloat16 [512, 4096], P(None, 'seq'), may hold values from -2.5 to 2.5
- cross_wq: bfloat16 [4096, 4096], P('seq', 'head')
- cross_wk: bfloat16 [2048, 4096], P(None, 'head'), may hold values from -0.125 to 0.125
- cross_wv: bfloat16 [2048, 4096], P(None, 'head'), may hold values from -0.125 to 0.125
- cross_wo: bfloat16 [4096, 4096], P('head', 'seq'), may hold values from -0.09375 to 0.09375
- self_wq: bfloat16 [4096, 4096], P('seq', 'head')
- self_wk: bfloat16 [4096, 4096], P('seq', 'head'), may hold values from -0.09375 to 0.09375
- self_wv: bfloat16 [4096, 4096], P('seq', 'head'), may hold values from -0.09375 to 0.09375
- self_wo: bfloat16 [4096, 4096], P('head', 'seq'), may hold values from -0.09375 to 0.09375
- cotangent: bfloat16 [512, 4096], P(None, 'seq'), may hold values from -6 to 6
Outputs:
- out_latents: float32 [512, 4096], P(None, 'seq')
- grad_w_q: float32 [4096, 4096], P('seq', 'head')
- grad_w_k: float32 [2048, 4096], P('seq', 'head')
- grad_w_v: float32 [2048, 4096], P('seq', 'head')
The draws below stay inside these ranges and needn't reach their ends.
Inputs may be any that keep to these rules, and one draw needn't show every extreme that they name: `prefix_len`: never falls from one latent to the next; the last latent's is 32768.
All inputs are finite; a program needn't handle non-finite values.
Results may differ from the reference program's by a relative error of at most 0.035.
Values may be sent and summed in bfloat16 or wider, within the bound.
A program may use at most 384 MiB of HBM per device.

```python
import math
import jax
import jax.numpy as jnp
import numpy as np
from jax import lax

E = 2048
LW = 4096
H = 32
HS = 128
VOCAB = 256
L = 512
CTX = 32768
HD = 4096


def head_scaled(key, rows, heads, head_size, top):
    first, second = jax.random.split(key)
    base = jax.random.normal(first, (rows, heads * head_size), jnp.float32) / math.sqrt(rows)
    logs = jax.random.uniform(second, (heads,), jnp.float32, 0.0, math.log(top))
    factor = jnp.repeat(jnp.exp(logs), head_size)
    return base * factor[None, :]


def draw_prefix_len(key, part):
    key = jax.random.fold_in(key, 1)
    picks = jax.random.randint(key, (L,), 1, CTX + 1, dtype=jnp.int32)
    picks = jnp.sort(picks)
    return picks.at[L - 1].set(CTX)


def draw_cross_wq(key, part):
    key = jax.random.fold_in(key, 2)
    top = 1.0
    return head_scaled(key, LW, H, HS, top).astype(jnp.bfloat16)


def draw_self_wq(key, part):
    key = jax.random.fold_in(key, 3)
    top = 1.0
    return head_scaled(key, LW, H, HS, top).astype(jnp.bfloat16)


def plant(result, rng, low, top_value):
    extent = result.shape
    index_at = [jax.random.randint(jax.random.fold_in(rng, axis), (), 0, extent[axis]) for axis in range(len(extent))]
    result = result.at[tuple(index_at)].set(low)
    longest = extent.index(max(extent))
    index_at[longest] = (index_at[longest] + 1) % extent[longest]
    return result.at[tuple(index_at)].set(top_value)


def steps_of(stream_key, shape, pieces, low, high):
    level, own = 1.0, jax.random.fold_in(stream_key, 6)
    for dim, blocks in pieces:
        draws = jnp.exp(jax.random.uniform(jax.random.fold_in(own, dim), (blocks,), jnp.float32, low / len(pieces), high / len(pieces)))
        level = level * jnp.repeat(draws, shape[dim] // blocks).reshape([-1 if axis == dim else 1 for axis in range(len(shape))])
    return level


def cumulative_ranks(number_of, lean):
    portions = [(1 << 20) // math.isqrt(grade ** lean) + 1 for grade in range(1, number_of + 1)]
    scale = 1 + sum(portions) // (1 << 30)
    return np.cumsum(np.array([max(1, weight // scale) for weight in portions]))


def skewed_ids(stream_key, extent, number_of, skew):
    table = cumulative_ranks(number_of, skew)
    ticket = jax.random.randint(jax.random.fold_in(stream_key, 1), extent, 0, int(table[number_of - 1]))
    rank = jnp.searchsorted(jnp.asarray(table, jnp.int32), ticket, side="right")
    return jax.random.permutation(jax.random.fold_in(stream_key, 2), number_of)[rank].astype(jnp.int32)


def bell_draw(stream_key, dims, spread, most, shards=(), kind=jnp.bfloat16):
    level = steps_of(stream_key, dims, shards, -0.22, 0.18) if shards else 1.0
    values = jax.random.normal(stream_key, dims, jnp.float32) * spread * level
    return jnp.minimum(jnp.maximum(values, -most), most).astype(kind)


def setup_inputs(seed: int = 0) -> dict:
    streams_of = jax.random.split(jax.random.key(seed), 14)
    return {
        "byte_ids": plant(skewed_ids(streams_of[0], (CTX,), VOCAB, 2), jax.random.fold_in(streams_of[0], 3), 0, VOCAB - 1).astype(jnp.int32),
        "prefix_len": draw_prefix_len(jax.random.fold_in(streams_of[13], 71), 0),
        "embed_table": bell_draw(streams_of[2], (VOCAB, E), 1.0, 6.0),
        "latents": bell_draw(streams_of[3], (L, LW), 0.5, 2.5, ((1, 32),)),
        "cross_wq": draw_cross_wq(jax.random.fold_in(streams_of[13], 71), 0),
        "cross_wk": bell_draw(streams_of[5], (E, HD), E ** -0.5, 0.125, ((1, 4),)),
        "cross_wv": bell_draw(streams_of[6], (E, HD), E ** -0.5, 0.125, ((1, 4),)),
        "cross_wo": bell_draw(streams_of[7], (HD, LW), HD ** -0.5, 0.09375, ((0, 4), (1, 32))),
        "self_wq": draw_self_wq(jax.random.fold_in(streams_of[13], 71), 0),
        "self_wk": bell_draw(streams_of[9], (LW, HD), LW ** -0.5, 0.09375, ((0, 32), (1, 4))),
        "self_wv": bell_draw(streams_of[10], (LW, HD), LW ** -0.5, 0.09375, ((0, 32), (1, 4))),
        "self_wo": bell_draw(streams_of[11], (HD, LW), HD ** -0.5, 0.09375, ((0, 4), (1, 32))),
        "cotangent": bell_draw(streams_of[12], (L, LW), 1.0, 6.0, ((1, 32),)),
    }


NEG = -1e+30

def rotate(x, pos, sign, head_size):
    count = x.shape[0]
    half = head_size // 2
    parts = x.reshape(count, -1, head_size)
    freq = jnp.exp(jnp.arange(half, dtype=jnp.float32) * (-math.log(10000.0) / half))
    angle = pos.astype(jnp.float32)[:, None] * freq[None, :]
    cosine = jnp.cos(angle)[:, None, :]
    sine = jnp.sin(angle)[:, None, :] * sign
    first = parts[..., :half]
    second = parts[..., half:]
    out = jnp.concatenate([first * cosine - second * sine, first * sine + second * cosine], axis=-1)
    return out.reshape(count, -1)

def normalize_rows(table):
    wide = table.astype(jnp.float32)
    return (wide * lax.rsqrt(lax.optimization_barrier(jnp.mean(wide * wide, axis=1, keepdims=True)) + 1e-06)).astype(jnp.bfloat16)

def reference(byte_ids, prefix_len, embed_table, latents, cross_wq, cross_wk, cross_wv, cross_wo, self_wq, self_wk, self_wv, self_wo, cotangent):
    scale = 1.0 / math.sqrt(HS)
    positions = jnp.arange(CTX, dtype=jnp.int32)
    normed = normalize_rows(embed_table)[byte_ids]
    live = positions[None, :] < prefix_len[:, None]
    stack_q = cross_wq.reshape(LW, H, HS).transpose(1, 0, 2)
    stack_k = cross_wk.reshape(E, H, HS).transpose(1, 0, 2)
    stack_v = cross_wv.reshape(E, H, HS).transpose(1, 0, 2)
    stack_o = cross_wo.reshape(H, HS, LW)

    def one_head(xs):
        wq_h, wk_h, wv_h, wo_h = xs
        q_raw = jnp.dot(latents, wq_h, preferred_element_type=jnp.float32)
        queries = (rotate(q_raw, prefix_len, 1.0, HS) * scale).astype(jnp.bfloat16)
        key_raw = jnp.dot(normed, wk_h, preferred_element_type=jnp.float32)
        keys = rotate(key_raw, positions, 1.0, HS).astype(jnp.bfloat16)
        values = jnp.dot(normed, wv_h, preferred_element_type=jnp.float32).astype(jnp.bfloat16)
        scores = jnp.dot(queries, keys.T, preferred_element_type=jnp.float32)
        row_max = lax.optimization_barrier(jnp.max(jnp.where(live, scores, NEG), axis=1))
        expo = jnp.where(live, jnp.exp(scores - row_max[:, None]), 0.0)
        totals = lax.optimization_barrier(jnp.sum(expo, axis=1))
        numer = jnp.dot(expo.astype(jnp.bfloat16), values, preferred_element_type=jnp.float32)
        attended = (numer / totals[:, None]).astype(jnp.bfloat16)
        log_total = row_max + jnp.log(totals)
        proj = jnp.dot(attended, wo_h, preferred_element_type=jnp.float32)
        grad_att = jnp.dot(cotangent, wo_h.T, preferred_element_type=jnp.float32).astype(jnp.bfloat16)
        delta = lax.optimization_barrier(jnp.sum(grad_att.astype(jnp.float32) * attended.astype(jnp.float32), axis=1))
        probs = jnp.where(live, jnp.exp(scores - log_total[:, None]), 0.0)
        grad_weights = jnp.dot(grad_att, values.T, preferred_element_type=jnp.float32)
        grad_scores = (probs * (grad_weights - delta[:, None])).astype(jnp.bfloat16)
        grad_values = jnp.dot(probs.astype(jnp.bfloat16).T, grad_att, preferred_element_type=jnp.float32).astype(jnp.bfloat16)
        key_grad = jnp.dot(grad_scores.T, queries, preferred_element_type=jnp.float32)
        grad_keys = rotate(key_grad, positions, -1.0, HS).astype(jnp.bfloat16)
        query_grad = jnp.dot(grad_scores, keys, preferred_element_type=jnp.float32)
        grad_queries = (rotate(query_grad, prefix_len, -1.0, HS) * scale).astype(jnp.bfloat16)
        gwq = jnp.dot(latents.T, grad_queries, preferred_element_type=jnp.float32)
        gwk = jnp.dot(normed.T, grad_keys, preferred_element_type=jnp.float32)
        gwv = jnp.dot(normed.T, grad_values, preferred_element_type=jnp.float32)
        return (proj, gwq, gwk, gwv)
    proj, gwq, gwk, gwv = lax.map(one_head, (stack_q, stack_k, stack_v, stack_o))
    state = (latents.astype(jnp.float32) + lax.optimization_barrier(jnp.sum(proj, axis=0))).astype(jnp.bfloat16)
    self_q = (jnp.dot(state, self_wq, preferred_element_type=jnp.float32) * scale).astype(jnp.bfloat16)
    self_k = jnp.dot(state, self_wk, preferred_element_type=jnp.float32).astype(jnp.bfloat16)
    self_v = jnp.dot(state, self_wv, preferred_element_type=jnp.float32).astype(jnp.bfloat16)
    cross_query_heads = self_q.reshape(L, H, HS).astype(jnp.float32)
    cross_key_heads = self_k.reshape(L, H, HS).astype(jnp.float32)
    cross_value_heads = self_v.reshape(L, H, HS).astype(jnp.float32)
    latent_scores = jnp.einsum('srv,brv->rsb', cross_query_heads, cross_key_heads)
    order = jnp.arange(L, dtype=jnp.int32)
    causal = order[:, None] >= order[None, :]
    self_max = lax.optimization_barrier(jnp.max(jnp.where(causal[None], latent_scores, NEG), axis=2, keepdims=True))
    latent_exponent = jnp.where(causal[None], jnp.exp(latent_scores - self_max), 0.0)
    self_tot = lax.optimization_barrier(jnp.sum(latent_exponent, axis=2))
    latent_numerator = jnp.einsum('yue,eyj->uyj', latent_exponent.astype(jnp.bfloat16).astype(jnp.float32), cross_value_heads)
    self_att = (latent_numerator / self_tot.T[:, :, None]).astype(jnp.bfloat16).reshape(L, HD)
    out_latents = state.astype(jnp.float32) + jnp.dot(self_att, self_wo, preferred_element_type=jnp.float32)
    grad_w_q = gwq.transpose(1, 0, 2).reshape(LW, HD)
    grad_w_k = gwk.transpose(1, 0, 2).reshape(E, HD)
    grad_w_v = gwv.transpose(1, 0, 2).reshape(E, HD)
    return (out_latents, grad_w_q, grad_w_k, grad_w_v)
```

```python
import math
import types

import jax
import jax.numpy as jnp
import numpy as np
from jax import lax
from jax.experimental import pallas as pl
from jax.experimental.pallas import tpu as pltpu
from jax.sharding import PartitionSpec as P

HS = 128
HALF = HS // 2
VOCAB = 256
NEG = -1e30
LOWEST = -1e29
QUADS = 4
BLOCK = 1024
ROWS = 128
LIMIT = 56 * 1024 * 1024
BF16 = jnp.bfloat16
F32 = jnp.float32


def frequencies():
    return np.exp(np.arange(HALF, dtype=np.float64) * (-math.log(10000.0) / HALF)).astype(np.float32)


def trig_tables(blocks):
    freq = frequencies().astype(np.float64)
    tiles = BLOCK // ROWS
    base = (
        np.arange(blocks * tiles)[None, :] * (QUADS * ROWS) + np.arange(QUADS)[:, None] * ROWS
    ).astype(np.float64)
    angle = base[:, :, None] * freq
    angle = angle.reshape(QUADS, blocks, tiles, HALF).transpose(0, 1, 3, 2)
    inner = freq[:, None] * np.arange(ROWS)[None, :]
    return [
        part.astype(np.float32) for part in (np.cos(angle), np.sin(angle), np.cos(inner), np.sin(inner))
    ]


def split_terms(x):
    high = x.astype(BF16)
    return high, (x - high.astype(F32)).astype(BF16)


def dot(a, b):
    return jnp.dot(a, b, preferred_element_type=F32)


def dot_nt(a, b):
    return lax.dot_general(a, b, (((1,), (1,)), ((), ())), preferred_element_type=F32)


def dot_tn(a, b):
    return lax.dot_general(a, b, (((0,), (0,)), ((), ())), preferred_element_type=F32)


def one_hot(ids):
    rows = lax.broadcasted_iota(jnp.int32, (VOCAB, ids.shape[1]), 0)
    return jnp.where(rows == ids, 1.0, 0.0).astype(BF16)


SIDE = 4
CORES = 2
CHIPS = SIDE * SIDE
AWAY = sorted(
    [(i, j) for i in range(SIDE) for j in range(SIDE) if i or j],
    key=lambda o: -(min(o[0], SIDE - o[0]) + min(o[1], SIDE - o[1])),
)
MESH = pl.DeviceIdType.MESH


class Place:
    def __init__(self):
        seq = lax.axis_index("seq")
        self.z = lax.axis_index("head")
        self.x = seq // (SIDE * CORES)
        self.y = (seq // CORES) % SIDE
        self.core = seq % CORES
        self.other = 1 - self.core

    def chip(self, i, j):
        return ((self.x + i) % SIDE) * SIDE + (self.y + j) % SIDE

    def device(self, i, j, core):
        return {"seq": self.chip(i, j) * CORES + core}

    def upper(self, z):
        return {"head": z}

    def quad_peers(self):
        near = self.y + 1 - 2 * (self.y % 2)
        chip, across = self.x * SIDE + self.y, self.x * SIDE + near
        low, high = self.y % 2, near % 2
        return [
            ({"seq": chip * CORES + self.other}, low * CORES + self.other),
            ({"seq": across * CORES + self.core}, high * CORES + self.core),
            ({"seq": across * CORES + self.other}, high * CORES + self.other),
        ]


def head_of(chip):
    return chip // 2


def quad_of(chip, core):
    return (chip % 2) * CORES + core


def lanes(index):
    return pl.ds(pl.multiple_of(index * HS, HS), HS)


def meet(peers):
    barrier = pltpu.get_barrier_semaphore()
    for peer in peers:
        pl.semaphore_signal(barrier, inc=1, device_id=peer, device_id_type=MESH)
    pl.semaphore_wait(barrier, len(peers))


def send(src, dst, sems, index, peer):
    copy = pltpu.make_async_remote_copy(
        src_ref=src,
        dst_ref=dst,
        send_sem=sems[0].at[index],
        recv_sem=sems[1].at[index],
        device_id=peer,
        device_id_type=MESH,
    )
    copy.start()
    return copy


TILES = BLOCK // ROWS


def block_trig(r, j, k):
    cb = r.cb[j][:, k : k + 1]
    sb = r.sb[j][:, k : k + 1]
    cc = r.cc[...]
    sc = r.sc[...]
    return cb * cc - sb * sc, sb * cc + cb * sc


def tile(k):
    return slice(k * ROWS, (k + 1) * ROWS)


def block_positions(j, quad):
    lane = lax.broadcasted_iota(jnp.int32, (1, BLOCK), 1)
    return j * (BLOCK * QUADS) + quad * ROWS + (lane // ROWS) * (QUADS * ROWS) + lane % ROWS


class Gather:
    def __init__(self, place, window, sems, pass_sems):
        self.place, self.window, self.pass_sems = place, window, pass_sems
        self.pair = place.device(0, 0, place.other)
        own = window(place.chip(0, 0), place.core)
        self.passed = [send(own, own, pass_sems, len(AWAY), self.pair)]
        self.away = [
            send(own, own, sems, n, place.device(i, j, place.core))
            for n, (i, j) in enumerate(AWAY)
        ]
        self.left = list(reversed(range(len(AWAY))))

    def forward(self, n):
        i, j = AWAY[n]
        self.left.remove(n)
        self.away[n].wait_recv()
        block = self.window(self.place.chip(SIDE - i, SIDE - j), self.place.core)
        copy = send(block, block, self.pass_sems, n, self.pair)
        self.passed.append(copy)
        return copy

    def forward_all(self):
        for n in list(self.left):
            self.forward(n)

    def arrive(self):
        for copy in self.passed:
            copy.wait_recv()

    def close(self):
        for copy in self.away + self.passed:
            copy.wait_send()


class Reduce:
    def __init__(self, place, piece, r, pair_sems, chip_sems):
        self.place, self.piece, self.r = place, piece, r
        pair = place.device(0, 0, place.other)
        self.pairs = []
        for n, (i, j) in enumerate(AWAY + [(0, 0)]):
            r.stage[n] = piece(place.chip(i, j), place.other).astype(r.stage.dtype)
            self.pairs.append(send(r.stage.at[n], r.pair_buf.at[n], pair_sems, n, pair))
        self.away = []
        for n, (i, j) in enumerate(AWAY):
            r.send_buf[n] = self.chip_sum(n, i, j).astype(BF16)
            self.away.append(
                send(
                    r.send_buf.at[n], r.recv_buf.at[n], chip_sems, n, place.device(i, j, place.core)
                )
            )

    def chip_sum(self, n, i, j):
        mine = self.piece(self.place.chip(i, j), self.place.core)
        self.pairs[n].wait_recv()
        return mine + self.r.pair_buf[n].astype(F32)

    def total(self):
        total = self.chip_sum(len(AWAY), 0, 0)
        for n in range(len(AWAY)):
            self.away[n].wait_recv()
            total = total + self.r.recv_buf[n].astype(F32)
        return total

    def close(self):
        for copy in self.away + self.pairs:
            copy.wait_send()


def plane_peers(place):
    return [place.device(i, j, place.core) for i, j in AWAY] + [
        place.device(0, 0, place.other),
        place.quad_peers()[2][0],
    ]


def turn(x, cosine, sine):
    u, w = x[:, :HALF], x[:, HALF:]
    return jnp.concatenate([u * cosine - w * sine, u * sine + w * cosine], axis=1)


def sum_heads(place, part, buf, stage, sems):
    copies = []
    for k in (2, 1, 3):
        to = (place.z + k) % SIDE
        stage[k - 1] = part(to).astype(stage.dtype)
        copies.append(send(stage.at[k - 1], buf.at[k - 1], sems, k - 1, place.upper(to)))
    return copies, part(place.z)


def summed(copies, total, buf):
    for copy in copies:
        copy.wait_recv()
    for k in range(SIDE - 1):
        total = total + buf[k].astype(F32)
    return total


def spread_heads(place, ref, sems):
    return [
        send(ref.at[place.z], ref.at[place.z], sems, k - 1, place.upper((place.z + k) % SIDE))
        for k in (2, 1, 3)
    ]


def head_peers(place):
    return [place.upper((place.z + k) % SIDE) for k in (2, 1, 3)]


def start_kernel(r):
    place = Place()
    chip = place.chip(0, 0)
    h, quad = head_of(chip), quad_of(chip, place.core)
    me = chip * CORES + place.core
    meet(plane_peers(place))
    columns = [
        pltpu.make_async_copy(src.at[:, lanes(h)], dst, r.wsem.at[n])
        for n, (src, dst) in enumerate([(r.wk, r.wk_own), (r.wv, r.wv_own)])
    ]
    for copy in columns:
        copy.start()
    r.all_ids[me] = r.ids[...]
    gather = Gather(
        place, lambda chip, core: r.all_ids.at[chip * CORES + core], (r.gs, r.gr), (r.fs, r.fr)
    )

    def piece(chip, core):
        h, q = head_of(chip), quad_of(chip, core)
        return jnp.concatenate(
            [dot(r.lat[q], r.wq[:, lanes(h)]), dot_nt(r.cot[q], r.wo[lanes(h)])], axis=1
        )

    reduce = Reduce(place, piece, r, (r.ps, r.pr), (r.cs, r.cr))

    wide = r.table[...].astype(F32)
    table = (wide * lax.rsqrt(jnp.mean(wide * wide, axis=1, keepdims=True) + 1e-06)).astype(BF16)
    r.normed[...] = table
    pair_columns = r.normed[:, lanes(chip)]
    r.own_table[...] = jnp.where(place.core == 0, pair_columns[:, :HALF], pair_columns[:, HALF:])
    for copy in columns:
        copy.wait()
    r.vtab[...] = dot(table, r.wv_own[...]).astype(BF16)
    high, low = split_terms(dot(table, r.wk_own[...]).T)
    r.ktab[:HS] = high
    r.ktab[HS:] = low

    gather.forward_all()
    gather.arrive()

    @pl.loop(0, r.kt.shape[0])
    def _(j):
        for k in range(TILES):
            ids = r.all_ids[j * QUADS + k // 2, pl.ds(quad + QUADS * (k % 2), 1), :]
            r.ids_out[j, :, tile(k)] = ids
            raw = dot(r.ktab[...], one_hot(ids))
            raw = raw[:HS] + raw[HS:]
            cosine, sine = block_trig(r, j, k)
            u, w = raw[:HALF], raw[HALF:]
            r.kt[j, :HALF, tile(k)] = (u * cosine - w * sine).astype(BF16)
            r.kt[j, HALF:, tile(k)] = (u * sine + w * cosine).astype(BF16)

    total = reduce.total()
    r.own[0] = (
        turn(total[:, :HS], r.cosine[...], r.sine[...]) * (1.0 / math.sqrt(HS))
    ).astype(BF16)
    r.own[1] = total[:, HS:].astype(BF16)
    quads = [
        send(r.own, r.out.at[:, quad], (r.qs, r.qr), n, peer)
        for n, (peer, _) in enumerate(place.quad_peers())
    ]
    r.out[:, quad] = r.own[...]
    for copy in quads:
        copy.wait()
    gather.close()
    reduce.close()


def forward_kernel(r):
    count = r.q.shape[0]
    chunks = count // ROWS
    r.m[...] = jnp.full(r.m.shape, LOWEST, F32)
    r.l[...] = jnp.zeros(r.l.shape, F32)
    r.hist[...] = jnp.zeros(r.hist.shape, F32)

    @pl.loop(0, r.kt.shape[0])
    def _(j):
        r.oh[...] = one_hot(r.ids[j])
        pos = block_positions(j, r.quad[0])

        def rows_from(start):
            for c in range(start, chunks):
                rows = slice(c * ROWS, (c + 1) * ROWS)
                s = dot(r.q[rows], r.kt[j])
                s = jnp.where(pos < r.pfx[rows], s, NEG)
                old = r.m[rows]
                new = jnp.maximum(old, jnp.max(s, axis=1, keepdims=True))
                alpha = jnp.exp(old - new)
                e = jnp.exp(s - new[:, :1])
                total = r.l[rows] * alpha
                for k in range(TILES):
                    total += e[:, tile(k)]
                r.l[rows] = total
                r.m[rows] = new
                r.hist[rows] = r.hist[rows] * alpha[:, :1] + dot_nt(e.astype(BF16), r.oh[...])

        for start in range(chunks):
            pl.when(r.first[j] == start)(lambda start=start: rows_from(start))

    total = jnp.maximum(jnp.sum(r.l[...], axis=1, keepdims=True), 1e-30)
    lse = r.m[...] + jnp.log(total)
    r.lse[...] = lse.T[:1]
    hist = r.hist[...] / total
    r.hist[...] = hist
    high, low = split_terms(hist)
    r.numer[...] = (dot(high, r.vtab[...]) + dot(low, r.vtab[...])).astype(BF16)


def back_blocks(r, quad, low, high):
    chunks = QUADS

    @pl.loop(low, high)
    def _(j):
        oh = one_hot(r.ids[j])
        r.oh[:VOCAB] = oh
        r.oh[VOCAB:] = oh
        pos = block_positions(j, quad)
        for c in range(chunks):
            rows = slice(c * ROWS, (c + 1) * ROWS)
            s = dot(r.q[rows], r.kt[j])
            s = jnp.where(pos < r.pfx[rows], s, NEG)
            p = jnp.exp(s - r.cols[rows, QUADS : QUADS + 1])
            ds = (p * dot(r.dmat[rows], r.oh[...])).astype(BF16)
            r.ds[rows] = ds
            r.dq[c] += dot_nt(ds, r.kt[j])
        grad = dot(r.qt[...], r.ds[...])
        for k in range(TILES):
            cosine, sine = block_trig(r, j, k)
            u, w = grad[:HALF, tile(k)], grad[HALF:, tile(k)]
            r.gkt[:HALF, tile(k)] = (u * cosine + w * sine).astype(BF16)
            r.gkt[HALF:, tile(k)] = (w * cosine - u * sine).astype(BF16)
        r.gk[...] += dot_nt(r.gkt[...], r.oh[:VOCAB])


def layer_kernel(r):
    place = Place()
    chip = place.chip(0, 0)
    h, quad = head_of(chip), quad_of(chip, place.core)
    quads = place.quad_peers()
    quarter = r.lat.shape[1]
    bins = VOCAB // QUADS
    closing = []
    meet(plane_peers(place) + head_peers(place))

    parts = []
    for n, (peer, rp) in enumerate(quads):
        parts.append(send(r.lse, r.lbuf.at[n], (r.ls, r.lr), n, peer))
        parts.append(send(r.numer.at[rp], r.nbuf.at[n], (r.ns, r.nr), n, peer))
    closing += parts
    r.gw[...] = dot_nt(r.ga[...].reshape(QUADS * quarter, HS), r.vtab[...])
    r.qt[...] = r.q[...].T
    r.dq[...] = jnp.zeros(r.dq.shape, F32)
    r.gk[...] = jnp.zeros(r.gk.shape, F32)
    for copy in parts:
        copy.wait_recv()
    terms = [r.lse[...]] + [r.lbuf[n] for n in range(QUADS - 1)]
    top = jnp.maximum(jnp.maximum(terms[0], terms[1]), jnp.maximum(terms[2], terms[3]))
    lse = top + jnp.log(sum(jnp.exp(t - top) for t in terms))
    r.flip[...] = jnp.zeros(r.flip.shape, F32)
    for n in range(QUADS):
        r.flip[pl.ds(n, 1)] = jnp.exp(terms[n] - lse)
    r.flip[pl.ds(QUADS, 1)] = lse
    r.cols[...] = r.flip[...].T
    share = r.cols[pl.ds(pl.multiple_of(quad * ROWS, ROWS), ROWS)]
    own = r.numer[quad].astype(F32) * share[:, :1]
    for n in range(QUADS - 1):
        own += r.nbuf[n].astype(F32) * share[:, n + 1 : n + 2]
    r.att[quad, :, lanes(h)] = own.astype(BF16)

    def att_window(chip, core):
        return r.att.at[quad_of(chip, core), :, lanes(head_of(chip))]

    gather = Gather(place, att_window, (r.gs, r.gr), (r.fs, r.fr))
    for j in (1, SIDE - 1):
        gather.forward(AWAY.index((0, j)))
    near, gather.passed = gather.passed, []
    for copy in near:
        copy.wait_recv()
    closing += near
    for c in range(QUADS):
        mine = r.att[c, :, lanes(h)].astype(F32)
        delta = jnp.sum(r.ga[c].astype(F32) * mine, axis=1, keepdims=True)
        high, low = split_terms(r.gw[tile(c)] - delta)
        r.dmat[tile(c), :VOCAB] = high
        r.dmat[tile(c), VOCAB:] = low
    back_blocks(r, quad, 0, 1)
    gather.forward_all()
    gather.arrive()

    zparts, total = sum_heads(
        place, lambda z: dot(r.att[z], r.cross_wo[...]), r.zbuf, r.zstage, (r.zs, r.zr)
    )
    back_blocks(r, quad, 1, 3)
    total = summed(zparts, total, r.zbuf)
    r.state[place.z] = (r.lat[place.z].astype(F32) + total).astype(BF16)
    spread = spread_heads(place, r.state, (r.ws, r.wr))
    back_blocks(r, quad, 3, 5)
    for copy in spread:
        copy.wait_recv()
    closing += spread + zparts

    def piece(chip, core):
        rows = r.state[quad_of(chip, core)]
        cols = lanes(head_of(chip))
        return jnp.concatenate(
            [dot(rows, w[:, cols]) for w in (r.self_wq, r.self_wk, r.self_wv)], axis=1
        )

    reduce = Reduce(place, piece, r, (r.ps, r.pr), (r.cs, r.cr))
    back_blocks(r, quad, 5, 8)
    grads = r.gk[...].T
    for c in range(QUADS):
        r.gstage[c, :bins] = grads[c * bins : (c + 1) * bins].astype(BF16)
    high, low = split_terms(r.hist[...] * r.cols[:, :1])
    ga = r.ga[...].reshape(QUADS * quarter, HS)
    grads = dot_tn(high, ga) + dot_tn(low, ga)
    for c in range(QUADS):
        r.gstage[c, bins:] = grads[c * bins : (c + 1) * bins].astype(BF16)
    total = reduce.total()
    self_q = (total[:, :HS] * (1.0 / math.sqrt(HS))).astype(BF16)
    r.own[0] = total[:, HS : 2 * HS].astype(BF16)
    r.own[1] = total[:, 2 * HS :].astype(BF16)
    kv = [
        send(r.own, r.kv.at[:, quad], (r.qs, r.qr), n, peer) for n, (peer, _) in enumerate(quads)
    ]
    r.kv[:, quad] = r.own[...]
    back = []
    for n, (peer, rp) in enumerate(quads):
        back.append(send(r.dq.at[rp], r.dbuf.at[n], (r.ds_s, r.ds_r), n, peer))
        back.append(send(r.gstage.at[rp], r.gbuf.at[n], (r.es, r.er), n, peer))
    for copy in kv:
        copy.wait_recv()
    closing += kv + back

    scores = dot_nt(self_q, r.kv[0].reshape(QUADS * quarter, HS))
    rows = quad * quarter + lax.broadcasted_iota(jnp.int32, scores.shape, 0)
    causal = rows >= lax.broadcasted_iota(jnp.int32, scores.shape, 1)
    scores = jnp.where(causal, scores, NEG)
    expo = jnp.exp(scores - jnp.max(scores, axis=1, keepdims=True))
    numer = dot(expo.astype(BF16), r.kv[1].reshape(QUADS * quarter, HS))
    r.att2[quad, :, lanes(h)] = (numer / jnp.sum(expo, axis=1, keepdims=True)).astype(BF16)

    def self_window(chip, core):
        return r.att2.at[quad_of(chip, core), :, lanes(head_of(chip))]

    again = Gather(place, self_window, (r.gs2, r.gr2), (r.fs2, r.fr2))

    for copy in back:
        copy.wait_recv()
    total = r.dq[quad]
    grads = r.gstage[quad].astype(F32)
    for n in range(QUADS - 1):
        total += r.dbuf[n]
        grads += r.gbuf[n].astype(F32)
    total = turn(total, r.cosine[...], -r.sine[...]) * (1.0 / math.sqrt(HS))
    r.comb[quad, :quarter, lanes(h)] = total.astype(BF16)
    r.comb[quad, quarter:, lanes(h)] = grads.astype(BF16)

    def comb_window(chip, core):
        return r.comb.at[quad_of(chip, core), :, lanes(head_of(chip))]

    last = Gather(place, comb_window, (r.gs3, r.gr3), (r.fs3, r.fr3))
    again.forward_all()
    again.arrive()

    zparts, total = sum_heads(
        place, lambda z: dot(r.att2[z], r.self_wo[...]), r.zbuf2, r.zstage2, (r.zs2, r.zr2)
    )
    last.forward_all()
    total = summed(zparts, total, r.zbuf2)
    r.out[place.z] = r.state[place.z].astype(F32) + total
    spread = spread_heads(place, r.out, (r.ws2, r.wr2))
    closing += zparts
    last.arrive()
    r.grad_q[...] = sum(dot_tn(r.lat[c], r.comb[c, :quarter]) for c in range(QUADS))
    for out, at in ((r.grad_k, quarter), (r.grad_v, quarter + bins)):
        out[...] = sum(
            dot_tn(r.own_table[c * bins : (c + 1) * bins], r.comb[c, at : at + bins])
            for c in range(QUADS)
        )
    for copy in spread:
        copy.wait()
    for copy in closing:
        copy.wait_send()
    for part in (gather, again, last, reduce):
        part.close()


def smem():
    return pl.BlockSpec(memory_space=pltpu.SMEM)


def vmem():
    return pl.BlockSpec(memory_space=pltpu.VMEM)


def anywhere():
    return pl.BlockSpec(memory_space=pl.ANY)


def shape(dims, kind=F32):
    return jax.ShapeDtypeStruct(dims, kind)


def call(kernel, ins, outs, scratch, collective_id=None, specs=()):
    names = list(ins) + list(outs) + list(scratch)
    specs = dict(specs)

    def run(*refs):
        kernel(types.SimpleNamespace(**dict(zip(names, refs))))

    extra = {}
    if collective_id is not None:
        extra = dict(collective_id=collective_id, has_side_effects=True)
    results = pl.pallas_call(
        run,
        out_shape=tuple(outs.values()),
        in_specs=[specs.get(name) or vmem() for name in ins],
        out_specs=tuple(vmem() for _ in outs),
        scratch_shapes=list(scratch.values()),
        compiler_params=pltpu.CompilerParams(vmem_limit_bytes=LIMIT, **extra),
        name=kernel.__name__,
    )(*ins.values())
    return types.SimpleNamespace(**dict(zip(outs, results)))


def gather_sems(tail=""):
    return {
        "gs" + tail: pltpu.SemaphoreType.DMA((CHIPS - 1,)),
        "gr" + tail: pltpu.SemaphoreType.DMA((CHIPS - 1,)),
        "fs" + tail: pltpu.SemaphoreType.DMA((CHIPS,)),
        "fr" + tail: pltpu.SemaphoreType.DMA((CHIPS,)),
    }


def reduce_scratch(quarter, wide, kind):
    return dict(
        stage=pltpu.VMEM((CHIPS, quarter, wide), kind),
        pair_buf=pltpu.VMEM((CHIPS, quarter, wide), kind),
        send_buf=pltpu.VMEM((CHIPS - 1, quarter, wide), BF16),
        recv_buf=pltpu.VMEM((CHIPS - 1, quarter, wide), BF16),
        own=pltpu.VMEM((2, quarter, HS), BF16),
        ps=pltpu.SemaphoreType.DMA((CHIPS,)),
        pr=pltpu.SemaphoreType.DMA((CHIPS,)),
        cs=pltpu.SemaphoreType.DMA((CHIPS - 1,)),
        cr=pltpu.SemaphoreType.DMA((CHIPS - 1,)),
        qs=pltpu.SemaphoreType.DMA((QUADS - 1,)),
        qr=pltpu.SemaphoreType.DMA((QUADS - 1,)),
    )


def on_device(
    byte_ids,
    prefix_len,
    embed_table,
    latents,
    cross_wq,
    cross_wk,
    cross_wv,
    cross_wo,
    self_wq,
    self_wk,
    self_wv,
    self_wo,
    cotangent,
):
    seq = lax.axis_index("seq")
    seqs = lax.axis_size("seq")
    quad = seq % QUADS
    n_lat = latents.shape[0]
    quarter = n_lat // QUADS
    width = cross_wq.shape[1]
    own_cols = latents.shape[1]
    blocks = byte_ids.shape[0] * seqs // QUADS // BLOCK
    bins = VOCAB // QUADS
    features = embed_table.shape[1] // seqs

    cb, sb, cc, sc = trig_tables(blocks)
    trig = dict(
        cb=lax.dynamic_index_in_dim(jnp.asarray(cb), quad, 0, keepdims=False),
        sb=lax.dynamic_index_in_dim(jnp.asarray(sb), quad, 0, keepdims=False),
        cc=jnp.asarray(cc),
        sc=jnp.asarray(sc),
    )
    own_prefix = lax.dynamic_slice_in_dim(prefix_len, quad * quarter, quarter, 0)
    angle = own_prefix.astype(F32)[:, None] * jnp.asarray(frequencies())[None, :]
    cosine, sine = jnp.cos(angle), jnp.sin(angle)
    lat_rows = latents.reshape(QUADS, quarter, own_cols)
    start = call(
        start_kernel,
        dict(
            ids=byte_ids.reshape(-1, ROWS),
            table=embed_table,
            wk=cross_wk,
            wv=cross_wv,
            lat=lat_rows,
            cot=cotangent.reshape(QUADS, quarter, own_cols),
            wq=cross_wq,
            wo=cross_wo,
            cosine=cosine,
            sine=sine,
            **trig,
        ),
        dict(
            out=shape((2, QUADS, quarter, HS), BF16),
            kt=shape((blocks, HS, BLOCK), BF16),
            ids_out=shape((blocks, 1, BLOCK), jnp.int32),
            vtab=shape((VOCAB, HS), BF16),
            own_table=shape((VOCAB, features), BF16),
        ),
        dict(
            all_ids=pltpu.VMEM((seqs, byte_ids.shape[0] // ROWS, ROWS), jnp.int32),
            normed=pltpu.VMEM(embed_table.shape, BF16),
            wk_own=pltpu.VMEM((embed_table.shape[1], HS), BF16),
            wv_own=pltpu.VMEM((embed_table.shape[1], HS), BF16),
            wsem=pltpu.SemaphoreType.DMA((2,)),
            ktab=pltpu.VMEM((2 * HS, VOCAB), BF16),
            **reduce_scratch(quarter, 2 * HS, F32),
            **gather_sems(),
        ),
        collective_id=0,
        specs=dict(wk=anywhere(), wv=anywhere()),
    )
    ga = start.out[1]
    q = start.out[0].reshape(n_lat, HS)

    starts = jnp.arange(blocks, dtype=jnp.int32) * (BLOCK * QUADS) + quad * ROWS
    first = jnp.sum((prefix_len[None, :] <= starts[:, None]).astype(jnp.int32), axis=1) // ROWS
    first = jnp.minimum(first, n_lat // ROWS - 1)
    pfx = prefix_len[:, None]
    ahead = call(
        forward_kernel,
        dict(
            first=first,
            quad=quad.astype(jnp.int32).reshape(1),
            q=q,
            kt=start.kt,
            ids=start.ids_out,
            pfx=pfx,
            vtab=start.vtab,
        ),
        dict(
            lse=shape((1, n_lat)), hist=shape((n_lat, VOCAB)), numer=shape((n_lat, HS), BF16)
        ),
        dict(
            m=pltpu.VMEM((n_lat, HS), F32),
            l=pltpu.VMEM((n_lat, HS), F32),
            oh=pltpu.VMEM((VOCAB, BLOCK), BF16),
        ),
        specs=dict(first=smem(), quad=smem()),
    )

    layer = call(
        layer_kernel,
        dict(
            lse=ahead.lse,
            hist=ahead.hist,
            numer=ahead.numer.reshape(QUADS, quarter, HS),
            q=q,
            ga=ga,
            kt=start.kt,
            ids=start.ids_out,
            pfx=pfx,
            vtab=start.vtab,
            own_table=start.own_table,
            lat=lat_rows,
            cosine=cosine,
            sine=sine,
            cross_wo=cross_wo,
            self_wq=self_wq,
            self_wk=self_wk,
            self_wv=self_wv,
            self_wo=self_wo,
            **trig,
        ),
        dict(
            out=shape((QUADS, quarter, own_cols)),
            grad_q=shape((own_cols, width)),
            grad_k=shape((features, width)),
            grad_v=shape((features, width)),
        ),
        dict(
            lbuf=pltpu.VMEM((QUADS - 1, 1, n_lat), F32),
            nbuf=pltpu.VMEM((QUADS - 1, quarter, HS), BF16),
            gw=pltpu.VMEM((n_lat, VOCAB), F32),
            qt=pltpu.VMEM((HS, n_lat), BF16),
            dq=pltpu.VMEM((QUADS, quarter, HS), F32),
            gk=pltpu.VMEM((HS, VOCAB), F32),
            flip=pltpu.VMEM((HS, n_lat), F32),
            cols=pltpu.VMEM((n_lat, HS), F32),
            att=pltpu.VMEM((QUADS, quarter, width), BF16),
            att2=pltpu.VMEM((QUADS, quarter, width), BF16),
            comb=pltpu.VMEM((QUADS, quarter + 2 * bins, width), BF16),
            dmat=pltpu.VMEM((n_lat, 2 * VOCAB), BF16),
            oh=pltpu.VMEM((2 * VOCAB, BLOCK), BF16),
            ds=pltpu.VMEM((n_lat, BLOCK), BF16),
            gkt=pltpu.VMEM((HS, BLOCK), BF16),
            state=pltpu.VMEM((QUADS, quarter, own_cols), BF16),
            zbuf=pltpu.VMEM((SIDE - 1, quarter, HS), BF16),
            zstage=pltpu.VMEM((SIDE - 1, quarter, HS), BF16),
            zbuf2=pltpu.VMEM((SIDE - 1, quarter, HS), BF16),
            zstage2=pltpu.VMEM((SIDE - 1, quarter, HS), BF16),
            gstage=pltpu.VMEM((QUADS, 2 * bins, HS), BF16),
            kv=pltpu.VMEM((2, QUADS, quarter, HS), BF16),
            dbuf=pltpu.VMEM((QUADS - 1, quarter, HS), F32),
            gbuf=pltpu.VMEM((QUADS - 1, 2 * bins, HS), BF16),
            **reduce_scratch(quarter, 3 * HS, BF16),
            **gather_sems(),
            **gather_sems("2"),
            **gather_sems("3"),
            **{
                name: pltpu.SemaphoreType.DMA((3,))
                for name in "ls lr ns nr zs zr ws wr zs2 zr2 ws2 wr2 ds_s ds_r es er".split()
            },
        ),
        collective_id=1,
    )
    return (layer.out.reshape(n_lat, own_cols), layer.grad_q, layer.grad_k, layer.grad_v)


def solution(mesh):
    return jax.shard_map(
        on_device,
        mesh=mesh,
        in_specs=(
            P("seq"),
            P(),
            P(),
            P(None, "seq"),
            P("seq", "head"),
            P(None, "head"),
            P(None, "head"),
            P("head", "seq"),
            P("seq", "head"),
            P("seq", "head"),
            P("seq", "head"),
            P("head", "seq"),
            P(None, "seq"),
        ),
        out_specs=(P(None, "seq"), P("seq", "head"), P("seq", "head"), P("seq", "head")),
        check_vma=False,
    )
```
